32 devices in a mesh: parts: 2 (over y), tiles: 8 (over z, x), mesh: 2 (over core).
Axes of the slice: x: 2, y: 2, z: 4, core: 2. Of those that a mesh axis runs over, the one named last changes fastest.
Arguments:
- patches: bfloat16 [1024, 128, 128], P(('parts', 'tiles', 'mesh')), parts along dimension 0, may hold values from -6 to 6
- send_index: int32 [32, 32], P(('parts', 'tiles', 'mesh')), parts along dimension 0, may hold values from 0 to 32, as said below
- pair_slots: int32 [32, 2, 16], P(('parts', 'tiles', 'mesh')), parts along dimension 0, may hold values from 0 to 32, as said below
- node_links: int32 [32, 4, 128], P(('parts', 'tiles', 'mesh')), parts along dimension 0, may hold values from 0 to 31
Outputs:
- pair_flow: float32 [2, 512], P(None, ('parts', 'tiles', 'mesh')), parts along dimension 1
- relaxed: float32 [2, 4096], P(None, ('parts', 'tiles', 'mesh')), parts along dimension 1
The draws below stay inside these ranges and needn't reach their ends.
There are 2 independent parts, one for each index of `parts`. The reference program is written for one: setup_inputs(seed, part) draws one part's arguments, and reference() takes and returns one part's arrays. A program takes and returns all parts, laid end to end along the dimension named above; each array names one. Nothing has to cross between parts.
Inputs may be any that keep to these rules, and one draw needn't show every extreme that they name: `send_index`: each patch is sent to at most one owner, as one side of one tile pair; a live pair's two sides come from two different tiles and pair_slots names their received slots, numbered source tile times 4 plus slot; the value 2 * 16 marks an empty send slot. Some device fills all 4 slots to one peer. `pair_slots`: the value 8 * 4 marks a pair slot without a live pair; the number of live pairs differs from owner to owner, and some owner has all 16 slots live.
All inputs are finite; a program needn't handle non-finite values.
Results may differ from the reference program's by a relative error of at most 0.011.
Values may be sent and summed in bfloat16 or wider, within the bound.
A program may use at most 64 MiB of HBM per device.

```python
import math
import jax
import jax.numpy as jnp
from jax import lax

PATCH = 128
PAIR_DEV = 16
NODE_DEV = 128
LINKS = 4
PATCHES_DEV = 32
DEVS = 16
N_TILES = 8
N_MESH = 2


def routing_tables(key):
    tile_count = N_TILES
    mesh_count = N_MESH
    pair_count = PAIR_DEV
    capacity = (2 * pair_count + tile_count - 1) // tile_count
    empty_patch = 2 * pair_count
    empty_slot = tile_count * capacity
    sides = jnp.arange(2 * pair_count, dtype=jnp.int32)
    owners = jnp.arange(tile_count, dtype=jnp.int32)
    base_key = jax.random.fold_in(key, 7)

    def one_column(column_key):
        keys = jax.random.split(column_key, 3)
        order = jax.random.permutation(keys[0], tile_count).astype(jnp.int32)
        offset = jax.random.permutation(keys[1], tile_count).astype(jnp.int32)
        counts = jax.random.randint(keys[2], (tile_count,), 3 * pair_count // 4, pair_count + 1).astype(jnp.int32)
        counts = counts.at[0].set(pair_count)
        places = (offset[:, None] + sides[None, :]) % tile_count
        sender = order[places]
        round_of = sides // tile_count
        pair_of = sides // 2
        live = pair_of[None, :] < counts[:, None]
        send_col = owners[:, None] * capacity + round_of[None, :]
        sends = jnp.full((tile_count, tile_count * capacity), empty_patch, jnp.int32)
        sends = sends.at[sender, send_col].set(jnp.where(live, sides[None, :], empty_patch))
        slot_value = jnp.where(live, sender * capacity + round_of[None, :], empty_slot)
        paired = slot_value.reshape(tile_count, pair_count, 2)
        slots = jnp.stack([paired[:, :, 1], paired[:, :, 0]], axis=1)
        return (sends, slots)
    column_keys = jax.vmap(lambda number: jax.random.fold_in(base_key, number))(jnp.arange(mesh_count, dtype=jnp.int32))
    sends, slots = jax.vmap(one_column)(column_keys)
    sends = jnp.swapaxes(sends, 0, 1).reshape(tile_count * mesh_count, tile_count * capacity)
    slots = jnp.swapaxes(slots, 0, 1).reshape(tile_count * mesh_count, 2, pair_count)
    return (sends.astype(jnp.int32), slots.astype(jnp.int32))


def draw_send_index(key, part):
    return routing_tables(key)[0]


def draw_pair_slots(key, part):
    return routing_tables(key)[1]


def touch_ends(array, key, least, largest):
    longest = array.shape.index(max(array.shape))
    spots = []
    for shift in (0, 1):
        where = [jax.random.randint(jax.random.fold_in(key, axis), (), 0, length) for axis, length in enumerate(array.shape)]
        where[longest] = (where[longest] + shift) % array.shape[longest]
        spots.append(tuple(where))
    return array.at[spots[0]].set(least).at[spots[1]].set(largest)


def level_of(own_key, dims, pieces, smallest, high):
    loudness = 1.0
    for position, blocks in pieces:
        draws = jax.random.uniform(jax.random.fold_in(jax.random.fold_in(own_key, 6), position), (blocks,), jnp.float32, smallest / len(pieces), high / len(pieces))
        loudness = loudness * jnp.repeat(jnp.exp(draws), dims[position] // blocks).reshape((-1,) + (1,) * (len(dims) - 1 - position))
    return loudness


def noise(stream_key, extent, spread, reach, cuts=(), held_as=jnp.bfloat16):
    loudness = level_of(stream_key, extent, cuts, -0.22, 0.18) if cuts else 1.0
    array = jax.random.normal(stream_key, extent, jnp.float32) * spread * loudness
    return jnp.minimum(jnp.maximum(array, -reach), reach).astype(held_as)


def setup_inputs(seed: int = 0, part: int = 0) -> dict:
    streams_of = jax.random.split(jax.random.key(seed), 5)
    part_keys = jax.random.split(jax.random.fold_in(streams_of[4], part), 5)
    return {
        "patches": noise(part_keys[0], (DEVS * PATCHES_DEV, PATCH, PATCH), 1.0, 6.0, ((0, 16),)),
        "send_index": draw_send_index(jax.random.fold_in(jax.random.fold_in(streams_of[4], part), 71), part),
        "pair_slots": draw_pair_slots(jax.random.fold_in(jax.random.fold_in(streams_of[4], part), 71), part),
        "node_links": touch_ends(jax.random.randint(part_keys[3], (DEVS, LINKS, NODE_DEV), 0, N_MESH * PAIR_DEV), jax.random.fold_in(part_keys[3], 1), 0, (N_MESH * PAIR_DEV) - 1).astype(jnp.int32),
    }


def make_tables(side_len):
    ticks = jnp.arange(side_len, dtype=jnp.int32)
    product = ticks[:, None] * ticks[None, :] % side_len
    angle = 2.0 * math.pi / side_len * product.astype(jnp.float32)
    cosine = jnp.cos(angle) / math.sqrt(side_len)
    sine = jnp.sin(angle) / math.sqrt(side_len)
    coord = ticks.astype(jnp.float32)
    gap = coord[:, None] - coord[None, :]
    narrow = jnp.exp(-gap * gap / (2.0 * 0.35 * 0.35)) / (0.35 * math.sqrt(2.0 * math.pi))
    broad = jnp.exp(-gap * gap / 32.0) / (4.0 * math.sqrt(2.0 * math.pi))
    band = narrow - broad
    lag = jnp.where(coord < side_len / 2, coord, coord - side_len)
    return (cosine.astype(jnp.bfloat16), sine.astype(jnp.bfloat16), band.astype(jnp.bfloat16), lag)

def high_dot(form, left, right):
    return jnp.einsum(form, left.astype(jnp.float32), right.astype(jnp.float32), precision=lax.Precision.HIGHEST)

def band_pass(stack, band):
    partial_value = high_dot('ij,bjk->bik', band, stack).astype(jnp.bfloat16)
    return high_dot('bij,kj->bik', partial_value, band).astype(jnp.bfloat16)

def spectral_flow(filtered, tables):
    cosine, sine, band, lag = tables
    side_len = filtered.shape[-1]
    count = filtered.shape[0] // 2
    left = jnp.concatenate([cosine, sine], 0)
    right = jnp.concatenate([cosine, sine], 1)
    back_left = jnp.concatenate([cosine, -sine], 1)
    halves = high_dot('ij,bjk->bik', left, filtered).astype(jnp.bfloat16)
    quarter = high_dot('bij,jk->bik', halves, right)
    real_part = quarter[:, :side_len, :side_len] - quarter[:, side_len:, side_len:]
    imag_part = -(quarter[:, :side_len, side_len:] + quarter[:, side_len:, :side_len])
    moving_real, fixed_real = (real_part[:count], real_part[count:])
    moving_imag, fixed_imag = (imag_part[:count], imag_part[count:])
    power_real = moving_real * fixed_real + moving_imag * fixed_imag
    power_imag = moving_imag * fixed_real - moving_real * fixed_imag
    power = jnp.concatenate([power_real, power_imag], 1).astype(jnp.bfloat16)
    mixed = high_dot('bij,jk->bik', power, right)
    first = mixed[:, :side_len, :side_len] - mixed[:, side_len:, side_len:]
    second = mixed[:, :side_len, side_len:] + mixed[:, side_len:, :side_len]
    stacked = jnp.concatenate([first, second], 1).astype(jnp.bfloat16)
    surface = high_dot('ij,bjk->bik', back_left, stacked)
    weight = surface * surface
    denom = lax.optimization_barrier(jnp.mean(weight, axis=(1, 2))) + 1e-06
    flow_y = lax.optimization_barrier(jnp.mean(lag[None, :, None] * weight, axis=(1, 2))) / denom
    flow_x = lax.optimization_barrier(jnp.mean(lag[None, None, :] * weight, axis=(1, 2))) / denom
    return jnp.stack([flow_y, flow_x], 0)

def reference(patches, send_index, pair_slots, node_links):
    tables = make_tables(PATCH)
    tile_count = N_TILES
    mesh_count = N_MESH
    pair_count = PAIR_DEV
    patch_count = 2 * pair_count
    capacity = send_index.shape[1] // tile_count
    empty_slot = tile_count * capacity
    devices = tile_count * mesh_count

    def owner_flows(owner):
        tile = owner // mesh_count
        lane = owner % mesh_count
        slots = pair_slots[owner]
        valid = slots < empty_slot
        safe = jnp.minimum(slots, empty_slot - 1)
        source = (safe // capacity * mesh_count + lane).astype(jnp.int32)
        local = send_index[source, tile * capacity + safe % capacity]
        valid = valid & (local < patch_count)
        flat = (source * patch_count + jnp.minimum(local, patch_count - 1)).astype(jnp.int32)
        chosen = patches[flat.reshape(-1)]
        chosen = jnp.where(valid.reshape(-1)[:, None, None], chosen, jnp.zeros_like(chosen))
        filtered = band_pass(chosen, tables[2])
        return spectral_flow(filtered, tables)
    all_flows = lax.map(owner_flows, jnp.arange(devices, dtype=jnp.int32))
    pair_flow = jnp.transpose(all_flows, (1, 0, 2)).reshape(2, devices * pair_count)
    group = all_flows.reshape(tile_count, mesh_count, 2, pair_count)
    group = jnp.transpose(group, (0, 2, 1, 3)).reshape(tile_count, 2, mesh_count * pair_count)
    tile_of = jnp.arange(devices, dtype=jnp.int32) // mesh_count

    def relax_one(flow_rows, links):
        linked = flow_rows[:, links]
        return 0.5 * linked[:, 0] + 0.5 * lax.optimization_barrier(jnp.mean(linked[:, 1:], axis=1))
    relaxed = jax.vmap(relax_one)(group[tile_of], node_links)
    relaxed = jnp.transpose(relaxed, (1, 0, 2)).reshape(2, devices * NODE_DEV)
    return (pair_flow, relaxed)
```

```python
import functools
import math

import jax
import jax.numpy as jnp
import ml_dtypes
import numpy as np
from jax import lax
from jax.experimental import pallas as pl
from jax.experimental.pallas import tpu as pltpu
from jax.sharding import PartitionSpec as P

MESH = pl.DeviceIdType.MESH
BF16 = jnp.bfloat16
F32 = jnp.float32


def make_tables(side_len):
    ticks = np.arange(side_len)
    product = ticks[:, None] * ticks[None, :] % side_len
    angle = np.float32(2.0 * math.pi / side_len) * product.astype(np.float32)
    root = math.sqrt(side_len)
    cosine = (np.cos(angle) / root).astype(np.float32).astype(ml_dtypes.bfloat16)
    sine = (np.sin(angle) / root).astype(np.float32).astype(ml_dtypes.bfloat16)
    coord = ticks.astype(np.float32)
    gap = coord[:, None] - coord[None, :]
    narrow = np.exp(-gap * gap / (2.0 * 0.35 * 0.35)) / (0.35 * math.sqrt(2.0 * math.pi))
    broad = np.exp(-gap * gap / 32.0) / (4.0 * math.sqrt(2.0 * math.pi))
    band = (narrow - broad).astype(np.float32).astype(ml_dtypes.bfloat16)
    lag = np.where(coord < side_len / 2, coord, coord - side_len).astype(np.float32)
    return cosine, sine, band, lag


def other_of(me, step, count):
    if count & (count - 1):
        raise ValueError("tiles: not 2**n")
    partner = 0
    bit = 1
    while bit < count:
        partner = partner + (me // bit + step // bit) % 2 * bit
        bit *= 2
    return partner


def dot(left, right):
    return jnp.dot(left, right, preferred_element_type=F32)


def kernel(
    tile_count,
    mesh_count,
    send_index,
    pair_slots,
    links,
    patches_hbm,
    band_hbm,
    left_hbm,
    right_hbm,
    back_hbm,
    final_hbm,
    lag_hbm,
    pair_out,
    relaxed_out,
    patches,
    band,
    left,
    right,
    back,
    final,
    lag,
    stage,
    recv,
    spectrum,
    sums,
    flows,
    load_sem,
    send_sem,
    recv_sem,
    flow_send_sem,
    flow_recv_sem,
):
    me = lax.axis_index("tiles")
    lane = lax.axis_index("mesh")
    patch_count = patches.shape[0]
    side = patches.shape[-1]
    slot_total = recv.shape[0]
    capacity = slot_total // tile_count
    pair_count = pair_slots.shape[-1]

    fetch = [
        pltpu.make_async_copy(src, dst, load_sem.at[n])
        for n, (src, dst) in enumerate(
            (
                (patches_hbm, patches),
                (band_hbm, band),
                (left_hbm, left),
                (right_hbm, right),
                (back_hbm, back),
                (final_hbm, final),
                (lag_hbm, lag),
            )
        )
    ]
    for copy in fetch:
        copy.start()

    barrier = pltpu.get_barrier_semaphore()

    def greet(step, carry):
        pl.semaphore_signal(
            barrier, inc=1, device_id={"tiles": other_of(me, step, tile_count)}, device_id_type=MESH
        )
        return carry

    lax.fori_loop(1, tile_count, greet, 0)
    for hop in range(1, mesh_count):
        pl.semaphore_signal(
            barrier, inc=1, device_id={"mesh": lax.rem(lane + hop, mesh_count)}, device_id_type=MESH
        )
    fetch[0].wait()

    def picked(step, slot):
        index = send_index[0, other_of(me, step, tile_count) * capacity + slot]
        block = patches[jnp.minimum(index, patch_count - 1)]
        return jnp.where(index < patch_count, block, jnp.zeros_like(block))

    def sending(step):
        block = pl.ds(step * capacity, capacity)
        return pltpu.make_async_remote_copy(
            src_ref=stage.at[block],
            dst_ref=recv.at[block],
            send_sem=send_sem.at[step],
            recv_sem=recv_sem.at[step],
            device_id={"tiles": other_of(me, step, tile_count)},
            device_id_type=MESH,
        )

    def fill(step):
        for slot in range(capacity):
            stage[step * capacity + slot] = picked(step, slot)

    fill(tile_count - 1)
    pl.semaphore_wait(barrier, tile_count + mesh_count - 2)
    sending(tile_count - 1).start()

    def send(turn, carry):
        step = tile_count - 1 - turn
        fill(step)
        sending(step).start()
        return carry

    lax.fori_loop(1, tile_count - 1, send, 0)
    for slot in range(capacity):
        recv[slot] = picked(0, slot)

    for copy in fetch[1:]:
        copy.wait()

    def prepare(step):
        blocks = [recv[step * capacity + slot] for slot in range(capacity)]
        width = 2 if capacity % 2 == 0 else 1
        for first in range(0, capacity, width):
            wide = jnp.concatenate(blocks[first : first + width], 1)
            partial = dot(band[...], wide).astype(BF16)
            tall = jnp.concatenate([partial[:, n * side : (n + 1) * side] for n in range(width)], 0)
            filtered = dot(tall, band[...]).astype(BF16)
            wide = jnp.concatenate([filtered[n * side : (n + 1) * side] for n in range(width)], 1)
            halves = dot(left[...], wide).astype(BF16)
            for n in range(width):
                columns = halves[:, n * side : (n + 1) * side]
                both = jnp.concatenate([columns[:side], columns[side:]], 1)
                spectrum[step * capacity + first + n] = dot(both, right[...])

    prepare(0)
    half = tile_count // 2

    def take(turn, carry):
        step = jnp.where(turn < half, turn, tile_count - 1 - (turn - half))
        sending(step).wait_recv()
        prepare(step)
        return carry

    lax.fori_loop(1, tile_count, take, 0)

    def place(slot):
        return other_of(me, slot // capacity, tile_count) * capacity + slot % capacity

    group = 2 if pair_count % 2 == 0 else 1

    def finish(turn, carry):
        backs = []
        lives = []
        for n in range(group):
            pair = turn * group + n
            moving_slot = pair_slots[0, 0, pair]
            fixed_slot = pair_slots[0, 1, pair]
            live = jnp.logical_and(moving_slot < slot_total, fixed_slot < slot_total)
            lives.append(jnp.where(live, 1.0, 0.0).astype(F32))
            moving = spectrum[place(jnp.minimum(moving_slot, slot_total - 1))]
            fixed = spectrum[place(jnp.minimum(fixed_slot, slot_total - 1))]
            mr, mi = moving[:, :side], moving[:, side:]
            fr, fi = fixed[:, :side], fixed[:, side:]
            power = jnp.concatenate([mr * fr + mi * fi, mi * fr - mr * fi], 1).astype(BF16)
            mixed = dot(power, back[...]).astype(BF16)
            backs.append(jnp.concatenate([mixed[:, :side], mixed[:, side:]], 0))
        surface = dot(final[...], jnp.concatenate(backs, 1))
        weight = surface * surface
        for n in range(group):
            part = weight[:, n * side : (n + 1) * side]
            pair = turn * group + n
            sums[0, pl.ds(pair, 1), :] = lives[n] * jnp.sum(part, axis=0, keepdims=True)
            sums[1, pl.ds(pair, 1), :] = lives[n] * jnp.sum(lag[:side] * part, axis=0, keepdims=True)
        return carry

    lax.fori_loop(0, pair_count // group, finish, 0)

    scale = 1.0 / (side * side)
    total = sums[0]
    denom = jnp.sum(total, axis=1, keepdims=True) * scale + 1e-06
    flow_y = jnp.sum(sums[1], axis=1, keepdims=True) * scale / denom
    flow_x = jnp.sum(total * lag[side : side + 1], axis=1, keepdims=True) * scale / denom
    own = [jnp.broadcast_to(flow_y, (pair_count, side)), jnp.broadcast_to(flow_x, (pair_count, side))]
    flows[lane, 0] = own[0]
    flows[lane, 1] = own[1]
    exchange = [
        pltpu.make_async_remote_copy(
            src_ref=flows.at[lane],
            dst_ref=flows.at[lane],
            send_sem=flow_send_sem.at[hop],
            recv_sem=flow_recv_sem.at[hop],
            device_id={"mesh": lax.rem(lane + hop, mesh_count)},
            device_id_type=MESH,
        )
        for hop in range(1, mesh_count)
    ]
    for copy in exchange:
        copy.start()
    rows = lax.broadcasted_iota(jnp.int32, (pair_count, side), 0)
    columns = lax.broadcasted_iota(jnp.int32, (pair_count, side), 1)
    for axis in range(2):
        line = jnp.sum(jnp.where(rows == columns, own[axis], 0.0), axis=0, keepdims=True)
        pair_out[pl.ds(axis, 1), :] = line[:, :pair_count]

    nodes = links.shape[-1]
    link_count = links.shape[1]
    rows = lax.broadcasted_iota(jnp.int32, (mesh_count * pair_count, nodes), 0)
    shares = jnp.where(rows == links[0, 0:1, :], 0.5, 0.0)
    for number in range(1, link_count):
        hit = rows == links[0, number : number + 1, :]
        shares = shares + jnp.where(hit, 0.5 / (link_count - 1), 0.0)
    for copy in exchange:
        copy.wait()
    for axis in range(2):
        line = jnp.zeros((1, nodes), F32)
        for number in range(mesh_count):
            part = shares[number * pair_count : (number + 1) * pair_count]
            line = line + jnp.sum(part * flows[number, axis][:, :nodes], axis=0, keepdims=True)
        relaxed_out[pl.ds(axis, 1), :] = line

    def drain(step, carry):
        sending(step).wait_send()
        return carry

    lax.fori_loop(1, tile_count, drain, 0)


def per_device(patches, send_index, pair_slots, node_links):
    patch_count, side, _ = patches.shape
    slot_total = send_index.shape[1]
    pair_count = pair_slots.shape[-1]
    nodes = node_links.shape[-1]
    tile_count = lax.axis_size("tiles")
    mesh_count = lax.axis_size("mesh")
    cosine, sine, band, lag = make_tables(side)
    left = np.concatenate([cosine, sine], 0)
    right = np.block([[cosine, -sine], [-sine, -cosine]])
    back = np.block([[cosine, sine], [-sine, cosine]])
    final = np.concatenate([cosine, -sine], 1)
    lags = np.zeros((side + 8, side), np.float32)
    lags[:side] = lag[:, None]
    lags[side:] = lag[None, :]
    tables = [jnp.asarray(table) for table in (band, left, right, back, final, lags)]
    smem = pl.BlockSpec(memory_space=pltpu.SMEM)
    vmem = pl.BlockSpec(memory_space=pltpu.VMEM)
    hbm = pl.BlockSpec(memory_space=pl.ANY)
    scratch = [
        pltpu.VMEM(patches.shape, BF16),
        *[pltpu.VMEM(table.shape, table.dtype) for table in tables],
        pltpu.VMEM((slot_total, side, side), BF16),
        pltpu.VMEM((slot_total, side, side), BF16),
        pltpu.VMEM((slot_total, side, 2 * side), F32),
        pltpu.VMEM((2, pair_count, side), F32),
        pltpu.VMEM((mesh_count, 2, pair_count, side), F32),
        pltpu.SemaphoreType.DMA((1 + len(tables),)),
        pltpu.SemaphoreType.DMA((tile_count,)),
        pltpu.SemaphoreType.DMA((tile_count,)),
        pltpu.SemaphoreType.DMA((mesh_count,)),
        pltpu.SemaphoreType.DMA((mesh_count,)),
    ]
    return pl.pallas_call(
        functools.partial(kernel, tile_count, mesh_count),
        out_shape=(
            jax.ShapeDtypeStruct((2, pair_count), F32),
            jax.ShapeDtypeStruct((2, nodes), F32),
        ),
        in_specs=[smem, smem, vmem, hbm] + [hbm] * len(tables),
        out_specs=(vmem, vmem),
        scratch_shapes=scratch,
        compiler_params=pltpu.CompilerParams(
            collective_id=0, has_side_effects=True, vmem_limit_bytes=48 * 2**20
        ),
        name="flow",
    )(send_index, pair_slots, node_links, patches, *tables)


def solution(mesh):
    spread = ("parts", "tiles", "mesh")
    placed = (
        P(spread, None, None),
        P(spread, None),
        P(spread, None, None),
        P(spread, None, None),
    )
    return jax.shard_map(
        per_device,
        mesh=mesh,
        in_specs=placed,
        out_specs=(P(None, spread), P(None, spread)),
        check_vma=False,
    )
```

```python
import functools
import math

import jax
import jax.numpy as jnp
import ml_dtypes
import numpy as np
from jax import lax
from jax.experimental import pallas as pl
from jax.experimental.pallas import tpu as pltpu
from jax.sharding import PartitionSpec as P

MESH = pl.DeviceIdType.MESH
BF16 = jnp.bfloat16
F32 = jnp.float32


def make_tables(side_len):
    ticks = np.arange(side_len)
    product = ticks[:, None] * ticks[None, :] % side_len
    angle = np.float32(2.0 * math.pi / side_len) * product.astype(np.float32)
    root = math.sqrt(side_len)
    cosine = (np.cos(angle) / root).astype(np.float32).astype(ml_dtypes.bfloat16)
    sine = (np.sin(angle) / root).astype(np.float32).astype(ml_dtypes.bfloat16)
    coord = ticks.astype(np.float32)
    gap = coord[:, None] - coord[None, :]
    narrow = np.exp(-gap * gap / (2.0 * 0.35 * 0.35)) / (0.35 * math.sqrt(2.0 * math.pi))
    broad = np.exp(-gap * gap / 32.0) / (4.0 * math.sqrt(2.0 * math.pi))
    band = (narrow - broad).astype(np.float32).astype(ml_dtypes.bfloat16)
    lag = np.where(coord < side_len / 2, coord, coord - side_len).astype(np.float32)
    return cosine, sine, band, lag


def other_of(me, step, count):
    if count & (count - 1):
        raise ValueError("tiles: not 2**n")
    partner = 0
    bit = 1
    while bit < count:
        partner = partner + (me // bit + step // bit) % 2 * bit
        bit *= 2
    return partner


def dot(left, right):
    return jnp.dot(left, right, preferred_element_type=F32)


def kernel(
    tile_count,
    mesh_count,
    send_hbm,
    slots_hbm,
    links_hbm,
    patches_hbm,
    band_hbm,
    left_hbm,
    right_hbm,
    back_hbm,
    final_hbm,
    lag_hbm,
    pair_out,
    relaxed_out,
    send_index,
    pair_slots,
    links,
    patches,
    band,
    left,
    right,
    back,
    final,
    lag,
    stage,
    recv,
    spectrum,
    sums,
    flows,
    load_sem,
    send_sem,
    recv_sem,
    flow_send_sem,
    flow_recv_sem,
):
    me = lax.axis_index("tiles")
    lane = lax.axis_index("mesh")
    patch_count = patches.shape[0]
    side = patches.shape[-1]
    slot_total = recv.shape[0]
    capacity = slot_total // tile_count
    pair_count = pair_slots.shape[-1]

    fetch = [
        pltpu.make_async_copy(src, dst, load_sem.at[n])
        for n, (src, dst) in enumerate(
            (
                (patches_hbm, patches),
                (send_hbm, send_index),
                (slots_hbm, pair_slots),
                (links_hbm, links),
                (band_hbm, band),
                (left_hbm, left),
                (right_hbm, right),
                (back_hbm, back),
                (final_hbm, final),
                (lag_hbm, lag),
            )
        )
    ]
    for copy in fetch:
        copy.start()

    barrier = pltpu.get_barrier_semaphore()

    def greet(step, carry):
        pl.semaphore_signal(
            barrier, inc=1, device_id={"tiles": other_of(me, step, tile_count)}, device_id_type=MESH
        )
        return carry

    lax.fori_loop(1, tile_count, greet, 0)
    for hop in range(1, mesh_count):
        pl.semaphore_signal(
            barrier, inc=1, device_id={"mesh": lax.rem(lane + hop, mesh_count)}, device_id_type=MESH
        )
    fetch[0].wait()
    fetch[1].wait()

    def picked(step, slot):
        index = send_index[0, other_of(me, step, tile_count) * capacity + slot]
        block = patches[jnp.minimum(index, patch_count - 1)]
        return jnp.where(index < patch_count, block, jnp.zeros_like(block))

    def sending(step):
        block = pl.ds(step * capacity, capacity)
        return pltpu.make_async_remote_copy(
            src_ref=stage.at[block],
            dst_ref=recv.at[block],
            send_sem=send_sem.at[step],
            recv_sem=recv_sem.at[step],
            device_id={"tiles": other_of(me, step, tile_count)},
            device_id_type=MESH,
        )

    def fill(step):
        for slot in range(capacity):
            stage[step * capacity + slot] = picked(step, slot)

    fill(1)
    pl.semaphore_wait(barrier, tile_count + mesh_count - 2)
    sending(1).start()

    def send(step, carry):
        fill(step)
        sending(step).start()
        return carry

    lax.fori_loop(2, tile_count, send, 0)
    for slot in range(capacity):
        recv[slot] = picked(0, slot)

    for copy in fetch[2:]:
        copy.wait()

    def prepare(step):
        blocks = [recv[step * capacity + slot] for slot in range(capacity)]
        width = 2 if capacity % 2 == 0 else 1
        for first in range(0, capacity, width):
            wide = jnp.concatenate(blocks[first : first + width], 1)
            partial = dot(band[...], wide).astype(BF16)
            tall = jnp.concatenate([partial[:, n * side : (n + 1) * side] for n in range(width)], 0)
            filtered = dot(tall, band[...]).astype(BF16)
            wide = jnp.concatenate([filtered[n * side : (n + 1) * side] for n in range(width)], 1)
            halves = dot(left[...], wide).astype(BF16)
            for n in range(width):
                columns = halves[:, n * side : (n + 1) * side]
                both = jnp.concatenate([columns[:side], columns[side:]], 1)
                spectrum[step * capacity + first + n] = dot(both, right[...])

    prepare(0)

    def take(step, carry):
        sending(step).wait_recv()
        prepare(step)
        return carry

    lax.fori_loop(1, tile_count, take, 0)

    def place(slot):
        return other_of(me, slot // capacity, tile_count) * capacity + slot % capacity


    backs = []
    lives = []
    for pair in range(pair_count):
        moving_slot = pair_slots[0, 0, pair]
        fixed_slot = pair_slots[0, 1, pair]
        live = jnp.logical_and(moving_slot < slot_total, fixed_slot < slot_total)
        lives.append(jnp.where(live, 1.0, 0.0).astype(F32))
        moving = spectrum[place(jnp.minimum(moving_slot, slot_total - 1))]
        fixed = spectrum[place(jnp.minimum(fixed_slot, slot_total - 1))]
        mr, mi = moving[:, :side], moving[:, side:]
        fr, fi = fixed[:, :side], fixed[:, side:]
        power = jnp.concatenate([mr * fr + mi * fi, mi * fr - mr * fi], 1).astype(BF16)
        mixed = dot(power, back[...]).astype(BF16)
        backs.append(jnp.concatenate([mixed[:, :side], mixed[:, side:]], 0))
    for pair in range(pair_count):
        if pair % 2 == 0:
            surface = dot(final[...], jnp.concatenate(backs[pair : pair + 2], 1))
            weight = surface * surface
        part = weight[:, pair % 2 * side : (pair % 2 + 1) * side]
        sums[0, pair : pair + 1, :] = lives[pair] * jnp.sum(part, axis=0, keepdims=True)
        sums[1, pair : pair + 1, :] = lives[pair] * jnp.sum(lag[:side] * part, axis=0, keepdims=True)

    scale = 1.0 / (side * side)
    total = sums[0]
    denom = jnp.sum(total, axis=1, keepdims=True) * scale + 1e-06
    flow_y = jnp.sum(sums[1], axis=1, keepdims=True) * scale / denom
    flow_x = jnp.sum(total * lag[side : side + 1], axis=1, keepdims=True) * scale / denom
    own = [jnp.broadcast_to(flow_y, (pair_count, side)), jnp.broadcast_to(flow_x, (pair_count, side))]
    flows[lane, 0] = own[0]
    flows[lane, 1] = own[1]
    exchange = [
        pltpu.make_async_remote_copy(
            src_ref=flows.at[lane],
            dst_ref=flows.at[lane],
            send_sem=flow_send_sem.at[hop],
            recv_sem=flow_recv_sem.at[hop],
            device_id={"mesh": lax.rem(lane + hop, mesh_count)},
            device_id_type=MESH,
        )
        for hop in range(1, mesh_count)
    ]
    for copy in exchange:
        copy.start()
    rows = lax.broadcasted_iota(jnp.int32, (pair_count, side), 0)
    columns = lax.broadcasted_iota(jnp.int32, (pair_count, side), 1)
    for axis in range(2):
        line = jnp.sum(jnp.where(rows == columns, own[axis], 0.0), axis=0, keepdims=True)
        pair_out[pl.ds(axis, 1), :] = line[:, :pair_count]

    nodes = links.shape[-1]
    link_count = links.shape[1]
    rows = lax.broadcasted_iota(jnp.int32, (mesh_count * pair_count, nodes), 0)
    shares = jnp.where(rows == links[0, 0:1, :], 0.5, 0.0)
    for number in range(1, link_count):
        hit = rows == links[0, number : number + 1, :]
        shares = shares + jnp.where(hit, 0.5 / (link_count - 1), 0.0)
    for copy in exchange:
        copy.wait()
    for axis in range(2):
        line = jnp.zeros((1, nodes), F32)
        for number in range(mesh_count):
            part = shares[number * pair_count : (number + 1) * pair_count]
            line = line + jnp.sum(part * flows[number, axis][:, :nodes], axis=0, keepdims=True)
        relaxed_out[pl.ds(axis, 1), :] = line

    def drain(step, carry):
        sending(step).wait_send()
        return carry

    lax.fori_loop(1, tile_count, drain, 0)


def per_device(patches, send_index, pair_slots, node_links):
    patch_count, side, _ = patches.shape
    slot_total = send_index.shape[1]
    pair_count = pair_slots.shape[-1]
    nodes = node_links.shape[-1]
    tile_count = lax.axis_size("tiles")
    mesh_count = lax.axis_size("mesh")
    cosine, sine, band, lag = make_tables(side)
    left = np.concatenate([cosine, sine], 0)
    right = np.block([[cosine, -sine], [-sine, -cosine]])
    back = np.block([[cosine, sine], [-sine, cosine]])
    final = np.concatenate([cosine, -sine], 1)
    lags = np.zeros((side + 8, side), np.float32)
    lags[:side] = lag[:, None]
    lags[side:] = lag[None, :]
    tables = [jnp.asarray(table) for table in (band, left, right, back, final, lags)]
    vmem = pl.BlockSpec(memory_space=pltpu.VMEM)
    hbm = pl.BlockSpec(memory_space=pltpu.HBM)
    scratch = [
        pltpu.SMEM(send_index.shape, jnp.int32),
        pltpu.SMEM(pair_slots.shape, jnp.int32),
        pltpu.VMEM(node_links.shape, jnp.int32),
        pltpu.VMEM(patches.shape, BF16),
        *[pltpu.VMEM(table.shape, table.dtype) for table in tables],
        pltpu.VMEM((slot_total, side, side), BF16),
        pltpu.VMEM((slot_total, side, side), BF16),
        pltpu.VMEM((slot_total, side, 2 * side), F32),
        pltpu.VMEM((2, pair_count, side), F32),
        pltpu.VMEM((mesh_count, 2, pair_count, side), F32),
        pltpu.SemaphoreType.DMA((4 + len(tables),)),
        pltpu.SemaphoreType.DMA((tile_count,)),
        pltpu.SemaphoreType.DMA((tile_count,)),
        pltpu.SemaphoreType.DMA((mesh_count,)),
        pltpu.SemaphoreType.DMA((mesh_count,)),
    ]
    return pl.pallas_call(
        functools.partial(kernel, tile_count, mesh_count),
        out_shape=(
            jax.ShapeDtypeStruct((2, pair_count), F32),
            jax.ShapeDtypeStruct((2, nodes), F32),
        ),
        in_specs=[hbm] * (4 + len(tables)),
        out_specs=(vmem, vmem),
        scratch_shapes=scratch,
        compiler_params=pltpu.CompilerParams(
            collective_id=0, has_side_effects=True, vmem_limit_bytes=60 * 2**20
        ),
        name="flow",
    )(send_index, pair_slots, node_links, patches, *tables)


def solution(mesh):
    spread = ("parts", "tiles", "mesh")
    placed = (
        P(spread, None, None),
        P(spread, None),
        P(spread, None, None),
        P(spread, None, None),
    )
    return jax.shard_map(
        per_device,
        mesh=mesh,
        in_specs=placed,
        out_specs=(P(None, spread), P(None, spread)),
        check_vma=False,
    )
```

```python
import functools
import math

import jax
import jax.numpy as jnp
import ml_dtypes
import numpy as np
from jax import lax
from jax.experimental import pallas as pl
from jax.experimental.pallas import tpu as pltpu
from jax.sharding import PartitionSpec as P

MESH = pl.DeviceIdType.MESH
BF16 = jnp.bfloat16
F32 = jnp.float32


def make_tables(side_len):
    ticks = np.arange(side_len)
    product = ticks[:, None] * ticks[None, :] % side_len
    angle = np.float32(2.0 * math.pi / side_len) * product.astype(np.float32)
    root = math.sqrt(side_len)
    cosine = (np.cos(angle) / root).astype(np.float32).astype(ml_dtypes.bfloat16)
    sine = (np.sin(angle) / root).astype(np.float32).astype(ml_dtypes.bfloat16)
    coord = ticks.astype(np.float32)
    gap = coord[:, None] - coord[None, :]
    narrow = np.exp(-gap * gap / (2.0 * 0.35 * 0.35)) / (0.35 * math.sqrt(2.0 * math.pi))
    broad = np.exp(-gap * gap / 32.0) / (4.0 * math.sqrt(2.0 * math.pi))
    band = (narrow - broad).astype(np.float32).astype(ml_dtypes.bfloat16)
    lag = np.where(coord < side_len / 2, coord, coord - side_len).astype(np.float32)
    return cosine, sine, band, lag


def other_of(me, step, count):
    if count & (count - 1):
        raise ValueError("tiles: not 2**n")
    partner = 0
    bit = 1
    while bit < count:
        partner = partner + (me // bit + step // bit) % 2 * bit
        bit *= 2
    return partner


def dot(left, right):
    return jnp.dot(left, right, preferred_element_type=F32)


def kernel(
    tile_count,
    mesh_count,
    send_hbm,
    slots_hbm,
    links_hbm,
    patches_hbm,
    band_hbm,
    left_hbm,
    right_hbm,
    back_hbm,
    final_hbm,
    lag_hbm,
    out,
    send_index,
    pair_slots,
    links,
    patches,
    band,
    left,
    right,
    back,
    final,
    lag,
    stage,
    recv,
    spectrum,
    sums,
    flows,
    load_sem,
    send_sem,
    recv_sem,
    flow_send_sem,
    flow_recv_sem,
):
    me = lax.axis_index("tiles")
    lane = lax.axis_index("mesh")
    patch_count = patches.shape[0]
    side = patches.shape[-1]
    slot_total = recv.shape[0]
    capacity = slot_total // tile_count
    pair_count = pair_slots.shape[-1]

    barrier = pltpu.get_barrier_semaphore()

    def greet(turn, carry):
        step = tile_count - turn
        pl.semaphore_signal(
            barrier, inc=1, device_id={"tiles": other_of(me, step, tile_count)}, device_id_type=MESH
        )
        return carry

    lax.fori_loop(1, tile_count, greet, 0)
    for hop in range(1, mesh_count):
        pl.semaphore_signal(
            barrier, inc=1, device_id={"mesh": lax.rem(lane + hop, mesh_count)}, device_id_type=MESH
        )
    fetch = [
        pltpu.make_async_copy(src, dst, load_sem.at[n])
        for n, (src, dst) in enumerate(
            (
                (patches_hbm, patches),
                (send_hbm, send_index),
                (slots_hbm, pair_slots),
                (links_hbm, links),
                (band_hbm, band),
                (left_hbm, left),
                (right_hbm, right),
                (back_hbm, back),
                (final_hbm, final),
                (lag_hbm, lag),
            )
        )
    ]
    for copy in fetch:
        copy.start()

    fetch[0].wait()
    fetch[1].wait()

    def picked(step, slot):
        index = send_index[0, other_of(me, step, tile_count) * capacity + slot]
        block = patches[jnp.minimum(index, patch_count - 1)]
        return jnp.where(index < patch_count, block, jnp.zeros_like(block))

    pieces = 2 if capacity % 2 == 0 else 1
    piece = capacity // pieces

    def sending(step, part):
        block = pl.ds(step * capacity + part * piece, piece)
        return pltpu.make_async_remote_copy(
            src_ref=stage.at[block],
            dst_ref=recv.at[block],
            send_sem=send_sem.at[step, part],
            recv_sem=recv_sem.at[step, part],
            device_id={"tiles": other_of(me, step, tile_count)},
            device_id_type=MESH,
        )

    def fill(step):
        for slot in range(capacity):
            stage[step * capacity + slot] = picked(step, slot)

    fill(1)
    pl.semaphore_wait(barrier, tile_count + mesh_count - 2)
    for part in range(pieces):
        sending(1, part).start()

    def send(step, carry):
        fill(step)
        for part in range(pieces):
            sending(step, part).start()
        return carry

    lax.fori_loop(2, tile_count, send, 0)
    for slot in range(capacity):
        recv[slot] = picked(0, slot)

    for copy in fetch[2:]:
        copy.wait()

    def prepare(step, part):
        width = 2 if piece % 2 == 0 else 1
        for first in range(part * piece, part * piece + piece, width):
            blocks = [recv[step * capacity + first + n] for n in range(width)]
            wide = jnp.concatenate(blocks, 1)
            partial = dot(band[...], wide).astype(BF16)
            tall = jnp.concatenate([partial[:, n * side : (n + 1) * side] for n in range(width)], 0)
            filtered = dot(tall, band[...]).astype(BF16)
            wide = jnp.concatenate([filtered[n * side : (n + 1) * side] for n in range(width)], 1)
            halves = dot(left[...], wide).astype(BF16)
            for n in range(width):
                columns = halves[:, n * side : (n + 1) * side]
                both = jnp.concatenate([columns[:side], columns[side:]], 1)
                spectrum[step * capacity + first + n] = dot(both, right[...])

    for part in range(pieces):
        prepare(0, part)

    def take(step, carry):
        for part in range(pieces):
            sending(step, part).wait_recv()
            prepare(step, part)
        return carry

    lax.fori_loop(1, tile_count, take, 0)

    def place(slot):
        return other_of(me, slot // capacity, tile_count) * capacity + slot % capacity


    backs = []
    lives = []
    for pair in range(pair_count):
        moving_slot = pair_slots[0, 0, pair]
        fixed_slot = pair_slots[0, 1, pair]
        live = jnp.logical_and(moving_slot < slot_total, fixed_slot < slot_total)
        lives.append(jnp.where(live, 1.0, 0.0).astype(F32))
        moving = spectrum[place(jnp.minimum(moving_slot, slot_total - 1))]
        fixed = spectrum[place(jnp.minimum(fixed_slot, slot_total - 1))]
        mr, mi = moving[:, :side], moving[:, side:]
        fr, fi = fixed[:, :side], fixed[:, side:]
        power = jnp.concatenate([mr * fr + mi * fi, mi * fr - mr * fi], 1).astype(BF16)
        mixed = dot(power, back[...]).astype(BF16)
        backs.append(jnp.concatenate([mixed[:, :side], mixed[:, side:]], 0))
    for pair in range(pair_count):
        if pair % 2 == 0:
            surface = dot(final[...], jnp.concatenate(backs[pair : pair + 2], 1))
            weight = surface * surface
        part = weight[:, pair % 2 * side : (pair % 2 + 1) * side]
        sums[0, pair : pair + 1, :] = lives[pair] * jnp.sum(part, axis=0, keepdims=True)
        sums[1, pair : pair + 1, :] = lives[pair] * jnp.sum(lag[:side] * part, axis=0, keepdims=True)

    scale = 1.0 / (side * side)
    total = sums[0]
    denom = jnp.sum(total, axis=1, keepdims=True) * scale + 1e-06
    flow_y = jnp.sum(sums[1], axis=1, keepdims=True) * scale / denom
    flow_x = jnp.sum(total * lag[side : side + 1], axis=1, keepdims=True) * scale / denom
    own = [jnp.broadcast_to(flow_y, (pair_count, side)), jnp.broadcast_to(flow_x, (pair_count, side))]
    flows[lane, 0] = own[0]
    flows[lane, 1] = own[1]
    exchange = [
        pltpu.make_async_remote_copy(
            src_ref=flows.at[lane],
            dst_ref=flows.at[lane],
            send_sem=flow_send_sem.at[hop],
            recv_sem=flow_recv_sem.at[hop],
            device_id={"mesh": lax.rem(lane + hop, mesh_count)},
            device_id_type=MESH,
        )
        for hop in range(1, mesh_count)
    ]
    for copy in exchange:
        copy.start()
    rows = lax.broadcasted_iota(jnp.int32, (pair_count, side), 0)
    columns = lax.broadcasted_iota(jnp.int32, (pair_count, side), 1)
    for axis in range(2):
        line = jnp.sum(jnp.where(rows == columns, own[axis], 0.0), axis=0, keepdims=True)
        out[pl.ds(axis, 1), :] = line

    nodes = links.shape[-1]
    link_count = links.shape[1]
    rows = lax.broadcasted_iota(jnp.int32, (mesh_count * pair_count, nodes), 0)
    shares = jnp.where(rows == links[0, 0:1, :], 0.5, 0.0)
    for number in range(1, link_count):
        hit = rows == links[0, number : number + 1, :]
        shares = shares + jnp.where(hit, 0.5 / (link_count - 1), 0.0)
    for copy in exchange:
        copy.wait()
    for axis in range(2):
        line = jnp.zeros((1, nodes), F32)
        for number in range(mesh_count):
            part = shares[number * pair_count : (number + 1) * pair_count]
            line = line + jnp.sum(part * flows[number, axis][:, :nodes], axis=0, keepdims=True)
        out[pl.ds(2 + axis, 1), :] = line

    def drain(step, carry):
        for part in range(pieces):
            sending(step, part).wait_send()
        return carry

    lax.fori_loop(1, tile_count, drain, 0)


def split_outputs(both, pair_out, relaxed_out):
    pair_out[...] = both[0:2, : pair_out.shape[1]]
    relaxed_out[...] = both[2:4, :]


def per_device(patches, send_index, pair_slots, node_links):
    patch_count, side, _ = patches.shape
    slot_total = send_index.shape[1]
    pair_count = pair_slots.shape[-1]
    nodes = node_links.shape[-1]
    tile_count = lax.axis_size("tiles")
    mesh_count = lax.axis_size("mesh")
    cosine, sine, band, lag = make_tables(side)
    left = np.concatenate([cosine, sine], 0)
    right = np.block([[cosine, -sine], [-sine, -cosine]])
    back = np.block([[cosine, sine], [-sine, cosine]])
    final = np.concatenate([cosine, -sine], 1)
    lags = np.zeros((side + 8, side), np.float32)
    lags[:side] = lag[:, None]
    lags[side:] = lag[None, :]
    tables = [jnp.asarray(table) for table in (band, left, right, back, final, lags)]
    vmem = pl.BlockSpec(memory_space=pltpu.VMEM)
    hbm = pl.BlockSpec(memory_space=pltpu.HBM)
    scratch = [
        pltpu.SMEM(send_index.shape, jnp.int32),
        pltpu.SMEM(pair_slots.shape, jnp.int32),
        pltpu.VMEM(node_links.shape, jnp.int32),
        pltpu.VMEM(patches.shape, BF16),
        *[pltpu.VMEM(table.shape, table.dtype) for table in tables],
        pltpu.VMEM((slot_total, side, side), BF16),
        pltpu.VMEM((slot_total, side, side), BF16),
        pltpu.VMEM((slot_total, side, 2 * side), F32),
        pltpu.VMEM((2, pair_count, side), F32),
        pltpu.VMEM((mesh_count, 2, pair_count, side), F32),
        pltpu.SemaphoreType.DMA((4 + len(tables),)),
        pltpu.SemaphoreType.DMA((tile_count, 2)),
        pltpu.SemaphoreType.DMA((tile_count, 2)),
        pltpu.SemaphoreType.DMA((mesh_count,)),
        pltpu.SemaphoreType.DMA((mesh_count,)),
    ]
    both = pl.pallas_call(
        functools.partial(kernel, tile_count, mesh_count),
        out_shape=jax.ShapeDtypeStruct((4, nodes), F32),
        in_specs=[hbm] * (4 + len(tables)),
        out_specs=vmem,
        scratch_shapes=scratch,
        compiler_params=pltpu.CompilerParams(
            collective_id=0, has_side_effects=True, vmem_limit_bytes=60 * 2**20
        ),
        name="flow",
    )(send_index, pair_slots, node_links, patches, *tables)
    return pl.pallas_call(
        split_outputs,
        out_shape=(
            jax.ShapeDtypeStruct((2, pair_count), F32),
            jax.ShapeDtypeStruct((2, nodes), F32),
        ),
        in_specs=[vmem],
        out_specs=(vmem, vmem),
        name="split",
    )(both)


def solution(mesh):
    spread = ("parts", "tiles", "mesh")
    placed = (
        P(spread, None, None),
        P(spread, None),
        P(spread, None, None),
        P(spread, None, None),
    )
    return jax.shard_map(
        per_device,
        mesh=mesh,
        in_specs=placed,
        out_specs=(P(None, spread), P(None, spread)),
        check_vma=False,
    )
```

```python
import functools
import math

import jax
import jax.numpy as jnp
import ml_dtypes
import numpy as np
from jax import lax
from jax.experimental import pallas as pl
from jax.experimental.pallas import tpu as pltpu
from jax.sharding import PartitionSpec as P

MESH = pl.DeviceIdType.MESH
BF16 = jnp.bfloat16
F32 = jnp.float32


def make_tables(side_len):
    ticks = np.arange(side_len)
    product = ticks[:, None] * ticks[None, :] % side_len
    angle = np.float32(2.0 * math.pi / side_len) * product.astype(np.float32)
    root = math.sqrt(side_len)
    cosine = (np.cos(angle) / root).astype(np.float32).astype(ml_dtypes.bfloat16)
    sine = (np.sin(angle) / root).astype(np.float32).astype(ml_dtypes.bfloat16)
    coord = ticks.astype(np.float32)
    gap = coord[:, None] - coord[None, :]
    narrow = np.exp(-gap * gap / (2.0 * 0.35 * 0.35)) / (0.35 * math.sqrt(2.0 * math.pi))
    broad = np.exp(-gap * gap / 32.0) / (4.0 * math.sqrt(2.0 * math.pi))
    band = (narrow - broad).astype(np.float32).astype(ml_dtypes.bfloat16)
    lag = np.where(coord < side_len / 2, coord, coord - side_len).astype(np.float32)
    return cosine, sine, band, lag


def other_of(me, step, count):
    if count & (count - 1):
        raise ValueError("tiles: not 2**n")
    partner = 0
    bit = 1
    while bit < count:
        partner = partner + (me // bit + step // bit) % 2 * bit
        bit *= 2
    return partner


def dot(left, right):
    return jnp.dot(left, right, preferred_element_type=F32)


def kernel(
    tile_count,
    mesh_count,
    send_hbm,
    slots_hbm,
    links_hbm,
    patches_hbm,
    band_hbm,
    left_hbm,
    right_hbm,
    back_hbm,
    final_hbm,
    lag_hbm,
    out,
    send_index,
    pair_slots,
    links,
    patches,
    band,
    left,
    right,
    back,
    final,
    lag,
    stage,
    recv,
    spectrum,
    sums,
    flows,
    load_sem,
    send_sem,
    recv_sem,
    flow_send_sem,
    flow_recv_sem,
):
    me = lax.axis_index("tiles")
    lane = lax.axis_index("mesh")
    patch_count = patches.shape[0]
    side = patches.shape[-1]
    slot_total = recv.shape[0]
    capacity = slot_total // tile_count
    pair_count = pair_slots.shape[-1]

    barrier = pltpu.get_barrier_semaphore()

    def greet(turn, carry):
        step = tile_count - turn
        pl.semaphore_signal(
            barrier, inc=1, device_id={"tiles": other_of(me, step, tile_count)}, device_id_type=MESH
        )
        return carry

    lax.fori_loop(1, tile_count, greet, 0)
    for hop in range(1, mesh_count):
        pl.semaphore_signal(
            barrier, inc=1, device_id={"mesh": lax.rem(lane + hop, mesh_count)}, device_id_type=MESH
        )
    fetch = [
        pltpu.make_async_copy(src, dst, load_sem.at[n])
        for n, (src, dst) in enumerate(
            (
                (patches_hbm, patches),
                (send_hbm, send_index),
                (slots_hbm, pair_slots),
                (links_hbm, links),
                (band_hbm, band),
                (left_hbm, left),
                (right_hbm, right),
                (back_hbm, back),
                (final_hbm, final),
                (lag_hbm, lag),
            )
        )
    ]
    for copy in fetch:
        copy.start()

    fetch[0].wait()
    fetch[1].wait()

    def picked(step, slot):
        index = send_index[0, other_of(me, step, tile_count) * capacity + slot]
        block = patches[jnp.minimum(index, patch_count - 1)]
        return jnp.where(index < patch_count, block, jnp.zeros_like(block))

    pieces = 2 if capacity % 2 == 0 else 1
    piece = capacity // pieces

    def sending(step, part):
        block = pl.ds(step * capacity + part * piece, piece)
        return pltpu.make_async_remote_copy(
            src_ref=stage.at[block],
            dst_ref=recv.at[block],
            send_sem=send_sem.at[step, part],
            recv_sem=recv_sem.at[step, part],
            device_id={"tiles": other_of(me, step, tile_count)},
            device_id_type=MESH,
        )

    def fill(step):
        for slot in range(capacity):
            stage[step * capacity + slot] = picked(step, slot)

    fill(1)
    pl.semaphore_wait(barrier, tile_count + mesh_count - 2)
    for part in range(pieces):
        sending(1, part).start()

    def send(step, carry):
        fill(step)
        for part in range(pieces):
            sending(step, part).start()
        return carry

    lax.fori_loop(2, tile_count, send, 0)
    for slot in range(capacity):
        recv[slot] = picked(0, slot)

    for copy in fetch[2:]:
        copy.wait()

    def prepare(step, part):
        width = 2 if piece % 2 == 0 else 1
        for first in range(part * piece, part * piece + piece, width):
            blocks = [recv[step * capacity + first + n] for n in range(width)]
            wide = jnp.concatenate(blocks, 1)
            partial = dot(band[...], wide).astype(BF16)
            tall = jnp.concatenate([partial[:, n * side : (n + 1) * side] for n in range(width)], 0)
            filtered = dot(tall, band[...]).astype(BF16)
            wide = jnp.concatenate([filtered[n * side : (n + 1) * side] for n in range(width)], 1)
            halves = dot(left[...], wide).astype(BF16)
            for n in range(width):
                columns = halves[:, n * side : (n + 1) * side]
                both = jnp.concatenate([columns[:side], columns[side:]], 1)
                spectrum[step * capacity + first + n] = dot(both, right[...])

    for part in range(pieces):
        prepare(0, part)

    def take(step, carry):
        for part in range(pieces):
            sending(step, part).wait_recv()
            prepare(step, part)
        return carry

    lax.fori_loop(1, tile_count, take, 0)

    def place(slot):
        return other_of(me, slot // capacity, tile_count) * capacity + slot % capacity


    backs = []
    lives = []

    def settle(first):
        surface = dot(final[...], jnp.concatenate(backs[first : first + 2], 1))
        weight = surface * surface
        for pair in range(first, min(first + 2, pair_count)):
            part = weight[:, pair % 2 * side : (pair % 2 + 1) * side]
            sums[0, pair : pair + 1, :] = lives[pair] * jnp.sum(part, axis=0, keepdims=True)
            sums[1, pair : pair + 1, :] = lives[pair] * jnp.sum(lag[:side] * part, axis=0, keepdims=True)

    for pair in range(pair_count):
        moving_slot = pair_slots[0, 0, pair]
        fixed_slot = pair_slots[0, 1, pair]
        live = jnp.logical_and(moving_slot < slot_total, fixed_slot < slot_total)
        lives.append(jnp.where(live, 1.0, 0.0).astype(F32))
        moving = spectrum[place(jnp.minimum(moving_slot, slot_total - 1))]
        fixed = spectrum[place(jnp.minimum(fixed_slot, slot_total - 1))]
        mr, mi = moving[:, :side], moving[:, side:]
        fr, fi = fixed[:, :side], fixed[:, side:]
        power = jnp.concatenate([mr * fr + mi * fi, mi * fr - mr * fi], 1).astype(BF16)
        mixed = dot(power, back[...]).astype(BF16)
        backs.append(jnp.concatenate([mixed[:, :side], mixed[:, side:]], 0))
        if pair % 2 == 1 and pair >= 5:
            settle(pair - 5)
    for first in range(max(0, pair_count - 4 - pair_count % 2), pair_count, 2):
        settle(first)

    scale = 1.0 / (side * side)
    total = sums[0]
    denom = jnp.sum(total, axis=1, keepdims=True) * scale + 1e-06
    flow_y = jnp.sum(sums[1], axis=1, keepdims=True) * scale / denom
    flow_x = jnp.sum(total * lag[side : side + 1], axis=1, keepdims=True) * scale / denom
    own = [jnp.broadcast_to(flow_y, (pair_count, side)), jnp.broadcast_to(flow_x, (pair_count, side))]
    flows[lane, 0] = own[0]
    flows[lane, 1] = own[1]
    exchange = [
        pltpu.make_async_remote_copy(
            src_ref=flows.at[lane],
            dst_ref=flows.at[lane],
            send_sem=flow_send_sem.at[hop],
            recv_sem=flow_recv_sem.at[hop],
            device_id={"mesh": lax.rem(lane + hop, mesh_count)},
            device_id_type=MESH,
        )
        for hop in range(1, mesh_count)
    ]
    for copy in exchange:
        copy.start()
    rows = lax.broadcasted_iota(jnp.int32, (pair_count, side), 0)
    columns = lax.broadcasted_iota(jnp.int32, (pair_count, side), 1)
    for axis in range(2):
        line = jnp.sum(jnp.where(rows == columns, own[axis], 0.0), axis=0, keepdims=True)
        out[pl.ds(axis, 1), :] = line

    nodes = links.shape[-1]
    link_count = links.shape[1]
    rows = lax.broadcasted_iota(jnp.int32, (mesh_count * pair_count, nodes), 0)
    shares = jnp.where(rows == links[0, 0:1, :], 0.5, 0.0)
    for number in range(1, link_count):
        hit = rows == links[0, number : number + 1, :]
        shares = shares + jnp.where(hit, 0.5 / (link_count - 1), 0.0)
    for copy in exchange:
        copy.wait()
    for axis in range(2):
        line = jnp.zeros((1, nodes), F32)
        for number in range(mesh_count):
            part = shares[number * pair_count : (number + 1) * pair_count]
            line = line + jnp.sum(part * flows[number, axis][:, :nodes], axis=0, keepdims=True)
        out[pl.ds(2 + axis, 1), :] = line

    def drain(step, carry):
        for part in range(pieces):
            sending(step, part).wait_send()
        return carry

    lax.fori_loop(1, tile_count, drain, 0)


def split_outputs(both, pair_out, relaxed_out):
    pair_out[...] = both[0:2, : pair_out.shape[1]]
    relaxed_out[...] = both[2:4, :]


def per_device(patches, send_index, pair_slots, node_links):
    patch_count, side, _ = patches.shape
    slot_total = send_index.shape[1]
    pair_count = pair_slots.shape[-1]
    nodes = node_links.shape[-1]
    tile_count = lax.axis_size("tiles")
    mesh_count = lax.axis_size("mesh")
    cosine, sine, band, lag = make_tables(side)
    left = np.concatenate([cosine, sine], 0)
    right = np.block([[cosine, -sine], [-sine, -cosine]])
    back = np.block([[cosine, sine], [-sine, cosine]])
    final = np.concatenate([cosine, -sine], 1)
    lags = np.zeros((side + 8, side), np.float32)
    lags[:side] = lag[:, None]
    lags[side:] = lag[None, :]
    tables = [jnp.asarray(table) for table in (band, left, right, back, final, lags)]
    vmem = pl.BlockSpec(memory_space=pltpu.VMEM)
    hbm = pl.BlockSpec(memory_space=pltpu.HBM)
    scratch = [
        pltpu.SMEM(send_index.shape, jnp.int32),
        pltpu.SMEM(pair_slots.shape, jnp.int32),
        pltpu.VMEM(node_links.shape, jnp.int32),
        pltpu.VMEM(patches.shape, BF16),
        *[pltpu.VMEM(table.shape, table.dtype) for table in tables],
        pltpu.VMEM((slot_total, side, side), BF16),
        pltpu.VMEM((slot_total, side, side), BF16),
        pltpu.VMEM((slot_total, side, 2 * side), F32),
        pltpu.VMEM((2, pair_count, side), F32),
        pltpu.VMEM((mesh_count, 2, pair_count, side), F32),
        pltpu.SemaphoreType.DMA((4 + len(tables),)),
        pltpu.SemaphoreType.DMA((tile_count, 2)),
        pltpu.SemaphoreType.DMA((tile_count, 2)),
        pltpu.SemaphoreType.DMA((mesh_count,)),
        pltpu.SemaphoreType.DMA((mesh_count,)),
    ]
    both = pl.pallas_call(
        functools.partial(kernel, tile_count, mesh_count),
        out_shape=jax.ShapeDtypeStruct((4, nodes), F32),
        in_specs=[hbm] * (4 + len(tables)),
        out_specs=vmem,
        scratch_shapes=scratch,
        compiler_params=pltpu.CompilerParams(
            collective_id=0, has_side_effects=True, vmem_limit_bytes=60 * 2**20
        ),
        name="flow",
    )(send_index, pair_slots, node_links, patches, *tables)
    return pl.pallas_call(
        split_outputs,
        out_shape=(
            jax.ShapeDtypeStruct((2, pair_count), F32),
            jax.ShapeDtypeStruct((2, nodes), F32),
        ),
        in_specs=[vmem],
        out_specs=(vmem, vmem),
        name="split",
    )(both)


def solution(mesh):
    spread = ("parts", "tiles", "mesh")
    placed = (
        P(spread, None, None),
        P(spread, None),
        P(spread, None, None),
        P(spread, None, None),
    )
    return jax.shard_map(
        per_device,
        mesh=mesh,
        in_specs=placed,
        out_specs=(P(None, spread), P(None, spread)),
        check_vma=False,
    )
```
